256 devices in a mesh: row: 8 (over y, z_hi), col: 32 (over z_lo, x, core).
Axes of the slice: x: 4, y: 4, z: 8 (z_hi: 2, z_lo: 4; z = z_hi * 4 + z_lo), core: 2. Of those that a mesh axis runs over, the one named last changes fastest.
Arguments:
- tokens: bfloat16 [1024, 8192], P('col', 'row'), may hold values from -6 to 6
- w_gate: bfloat16 [8192, 28672], P('row', 'col'), may hold values from -0.0625 to 0.0625
- w_up: bfloat16 [8192, 28672], P('row', 'col'), may hold values from -0.0625 to 0.0625
- w_down: bfloat16 [28672, 8192], P('col', 'row'), may hold values from -0.03125 to 0.03125
- out_grad: bfloat16 [1024, 8192], P('col', 'row'), may hold values from -6 to 6
Outputs:
- mixed: bfloat16 [1024, 8192], P('col', 'row')
- in_grad: bfloat16 [1024, 8192], P('col', 'row')
- gate_grad: bfloat16 [8192, 28672], P('row', 'col')
- up_grad: bfloat16 [8192, 28672], P('row', 'col')
- down_grad: bfloat16 [28672, 8192], P('col', 'row')
The draws below stay inside these ranges and needn't reach their ends.
All inputs are finite; a program needn't handle non-finite values.
Results may differ from the reference program's by a relative error of at most 0.005.
Values may be sent and summed in bfloat16 or wider, within the bound.
No kernel may reach another device: no remote copies, remote signals or barrier semaphores. Data moves between devices by JAX's collectives and lax.ppermute only.
A program may use at most 128 MiB of HBM per device.

```python
import math
import jax
import jax.numpy as jnp

D = 8192
FF = 28672
TOKENS = 1024


def shard_levels(key, shape, pieces, least, largest):
    level = 1.0
    for position, blocks in pieces:
        steps = jax.random.uniform(jax.random.fold_in(jax.random.fold_in(key, 6), position), (blocks,), jnp.float32, least / len(pieces), largest / len(pieces))
        level = level * jnp.repeat(jnp.exp(steps), shape[position] // blocks).reshape((-1,) + (1,) * (len(shape) - 1 - position))
    return level


def bell_draw(stream_key, extent, deviation, limit, pieces=(), dtype=jnp.bfloat16):
    loudness = shard_levels(stream_key, extent, pieces, -0.22, 0.18) if pieces else 1.0
    entries = jax.random.normal(stream_key, extent, jnp.float32) * deviation * loudness
    return jnp.minimum(jnp.maximum(entries, -limit), limit).astype(dtype)


def setup_inputs(seed: int = 0) -> dict:
    key_of = jax.random.split(jax.random.key(seed), 6)
    return {
        "tokens": bell_draw(key_of[0], (TOKENS, D), 1.0, 6.0, ((0, 32), (1, 8))),
        "w_gate": bell_draw(key_of[1], (D, FF), D ** -0.5, 0.0625, ((0, 8), (1, 32))),
        "w_up": bell_draw(key_of[2], (D, FF), D ** -0.5, 0.0625, ((0, 8), (1, 32))),
        "w_down": bell_draw(key_of[3], (FF, D), FF ** -0.5, 0.03125, ((0, 32), (1, 8))),
        "out_grad": bell_draw(key_of[4], (TOKENS, D), 1.0, 6.0, ((0, 32), (1, 8))),
    }


def reference(tokens, w_gate, w_up, w_down, out_grad):
    gate_pre = jnp.dot(tokens, w_gate, preferred_element_type=jnp.float32)
    up_pre = jnp.dot(tokens, w_up, preferred_element_type=jnp.float32)
    sigmoid_g = jax.nn.sigmoid(gate_pre)
    activated = gate_pre * sigmoid_g
    hidden = (activated * up_pre).astype(jnp.bfloat16)
    mixed = jnp.dot(hidden, w_down, preferred_element_type=jnp.float32).astype(jnp.bfloat16)
    hid_grad = jnp.dot(out_grad, w_down.T, preferred_element_type=jnp.float32)
    gate_delta = (hid_grad * up_pre * sigmoid_g * (1.0 + gate_pre * (1.0 - sigmoid_g))).astype(jnp.bfloat16)
    up_delta = (hid_grad * activated).astype(jnp.bfloat16)
    in_grad = (jnp.dot(gate_delta, w_gate.T, preferred_element_type=jnp.float32) + jnp.dot(up_delta, w_up.T, preferred_element_type=jnp.float32)).astype(jnp.bfloat16)
    grad_scale = 1.0 / math.sqrt(TOKENS)
    gate_grad = (jnp.dot(tokens.T, gate_delta, preferred_element_type=jnp.float32) * grad_scale).astype(jnp.bfloat16)
    up_grad = (jnp.dot(tokens.T, up_delta, preferred_element_type=jnp.float32) * grad_scale).astype(jnp.bfloat16)
    down_grad = (jnp.dot(hidden.T, out_grad, preferred_element_type=jnp.float32) * grad_scale).astype(jnp.bfloat16)
    return (mixed, in_grad, gate_grad, up_grad, down_grad)
```

```python
import math

import jax
import jax.numpy as jnp
from jax import lax
from jax.sharding import PartitionSpec as P

BF, F32 = jnp.bfloat16, jnp.float32
NX, NZ, NY = 4, 4, 4
COLS = [(z, x, k) for z in range(NZ) for x in range(NX) for k in range(2)]


def col_of(z, x, k):
    return ((z % NZ) * NX + x % NX) * 2 + k


def shift_x(a, d):
    return lax.ppermute(a, "col", [(col_of(*c), col_of(c[0], c[1] + d, c[2])) for c in COLS])


def shift_z(a, d):
    return lax.ppermute(a, "col", [(col_of(*c), col_of(c[0] + d, c[1], c[2])) for c in COLS])


def swap_core(a):
    return lax.ppermute(a, "col", [(c, c ^ 1) for c in range(32)])


def shift_y(a, d):
    return lax.ppermute(a, "row", [(r, (r + 2 * d) % 8) for r in range(8)])


def swap_zh(a):
    return lax.ppermute(a, "row", [(r, r ^ 1) for r in range(8)])


def col_gather(a):
    a = jnp.concatenate([a, shift_z(a, 1), shift_z(a, 2), shift_z(a, 3)], axis=0)
    a = jnp.concatenate([a, shift_x(a, 1), shift_x(a, -1), shift_x(a, 2)], axis=0)
    return jnp.concatenate([a, swap_core(a)], axis=0)


def col_reduce(a):
    half = a.shape[0] // 2
    a = a[:half] + swap_core(a[half:])
    n = half // NX
    s = a[n:].astype(BF)
    a = (
        a[:n]
        + shift_x(s[:n], -1).astype(F32)
        + shift_x(s[n : 2 * n], 1).astype(F32)
        + shift_x(s[2 * n :], 2).astype(F32)
    )
    n = n // NZ
    s = a[n:].astype(BF)
    return (
        a[:n]
        + shift_z(s[:n], -1).astype(F32)
        + shift_z(s[n : 2 * n], -2).astype(F32)
        + shift_z(s[2 * n :], -3).astype(F32)
    )


def row_reduce(term, y, zh):
    far = shift_y(term((y + 2) % NY).astype(BF), 2)
    up = shift_y(term((y + 1) % NY).astype(BF), 1)
    down = shift_y(term((y + 3) % NY).astype(BF), -1)
    total = term(y) + up.astype(F32) + down.astype(F32) + far.astype(F32)
    n = total.shape[0] // 2
    other = lax.dynamic_slice_in_dim(total, (1 - zh) * n, n, 0).astype(BF)
    own = lax.dynamic_slice_in_dim(total, zh * n, n, 0)
    return own + swap_zh(other).astype(F32)


def row_gather(a, y, zh):
    b = swap_zh(a)
    first = zh == 0
    a = jnp.concatenate([jnp.where(first, a, b), jnp.where(first, b, a)], axis=0)
    ring = [a, shift_y(a, -1), shift_y(a, 2), shift_y(a, 1)]
    n = a.shape[0]
    out = jnp.zeros((NY * n, a.shape[1]), a.dtype)
    for j in range(NY):
        out = lax.dynamic_update_slice_in_dim(out, ring[j], ((y + j) % NY) * n, 0)
    return out


def body(tokens, w_gate, w_up, w_down, out_grad):
    row = lax.axis_index("row")
    y, zh = row // 2, row % 2
    all_tok = col_gather(tokens)
    all_grad = col_gather(out_grad)
    tok_total = all_tok.shape[0]
    block = tok_total // NY
    half_width = w_gate.shape[1]
    w_both = jnp.concatenate([w_gate, w_up], axis=1)

    def front_term(q):
        return jnp.dot(
            lax.dynamic_slice_in_dim(all_tok, q * block, block, 0),
            w_both,
            preferred_element_type=F32,
        )

    def back_term(q):
        return lax.dot_general(
            lax.dynamic_slice_in_dim(all_grad, q * block, block, 0),
            w_down,
            (((1,), (1,)), ((), ())),
            preferred_element_type=F32,
        )

    gate_up = row_reduce(front_term, y, zh)
    hid_grad = row_reduce(back_term, y, zh)
    gate_pre = gate_up[:, :half_width]
    up_pre = gate_up[:, half_width:]
    sigmoid_g = jax.nn.sigmoid(gate_pre)
    activated = gate_pre * sigmoid_g
    hidden = (activated * up_pre).astype(BF)
    hid_all = row_gather(hidden, y, zh)
    gate_delta = (hid_grad * up_pre * sigmoid_g * (1.0 + gate_pre * (1.0 - sigmoid_g))).astype(BF)
    up_delta = (hid_grad * activated).astype(BF)
    delta_all = row_gather(jnp.concatenate([gate_delta, up_delta], axis=1), y, zh)

    mixed = col_reduce(jnp.dot(hid_all, w_down, preferred_element_type=F32)).astype(BF)
    in_grad = col_reduce(
        lax.dot_general(delta_all, w_both, (((1,), (1,)), ((), ())), preferred_element_type=F32)
    ).astype(BF)
    grad_scale = 1.0 / math.sqrt(tok_total)
    both_grad = (
        lax.dot_general(all_tok, delta_all, (((0,), (0,)), ((), ())), preferred_element_type=F32)
        * grad_scale
    )
    gate_grad = both_grad[:, :half_width].astype(BF)
    up_grad = both_grad[:, half_width:].astype(BF)
    down_grad = (
        lax.dot_general(hid_all, all_grad, (((0,), (0,)), ((), ())), preferred_element_type=F32)
        * grad_scale
    ).astype(BF)
    return (mixed, in_grad, gate_grad, up_grad, down_grad)


def solution(mesh):
    placed = (P("col", "row"), P("row", "col"), P("row", "col"), P("col", "row"), P("col", "row"))
    return jax.shard_map(
        body,
        mesh=mesh,
        in_specs=placed,
        out_specs=(
            P("col", "row"),
            P("col", "row"),
            P("row", "col"),
            P("row", "col"),
            P("col", "row"),
        ),
        check_vma=False,
    )
```

```python
import math

import jax
import jax.numpy as jnp
from jax import lax
from jax.experimental import pallas as pl
from jax.experimental.pallas import tpu as pltpu
from jax.sharding import PartitionSpec as P

BF, F32 = jnp.bfloat16, jnp.float32
NX, NZ, NY = 4, 4, 4
ORDER = (2, 1, 3, 0)
DEVICES = [
    (y, h, z, x, k)
    for y in range(NY)
    for h in range(2)
    for z in range(NZ)
    for x in range(NX)
    for k in range(2)
]


def flat(y, h, z, x, k):
    return ((y % NY) * 2 + h % 2) * 32 + ((z % NZ) * NX + x % NX) * 2 + k % 2


def permute(a, name, target):
    with jax.named_scope(name):
        return lax.ppermute(a, ("row", "col"), [(flat(*d), flat(*target(*d))) for d in DEVICES])


def shift_y(a, d, name):
    return permute(a, name + "_y", lambda y, h, z, x, k: (y ^ d, h, z, x, k))


def shift_z(a, d, name):
    return permute(a, name + "_z", lambda y, h, z, x, k: (y, h, z ^ d, x, k))


def swap_h(a, name):
    return permute(a, name + "_h", lambda y, h, z, x, k: (y, h + 1, z, x, k))


def swap_core(a, name):
    return permute(a, name + "_core", lambda y, h, z, x, k: (y, h, z, x, k + 1))


def shift_x(a, d, name):
    return permute(a, name + "_x", lambda y, h, z, x, k: (y, h, z, x ^ d, k))


def after(a, *earlier):
    return lax.optimization_barrier((a, *earlier))[0]


def add(*parts):
    total = parts[0].astype(F32)
    for p in parts[1:]:
        total = total + p.astype(F32)
    return total


def dot(a, b, ca, cb):
    return lax.dot_general(a, b, (((ca,), (cb,)), ((), ())), preferred_element_type=F32)


def stack(parts):
    n = parts[0].shape[0]
    out = jnp.zeros((n * len(parts), parts[0].shape[1]), parts[0].dtype)
    for i, p in enumerate(parts):
        out = lax.dynamic_update_slice(out, p, (i * n, 0))
    return out


def places(y):
    place = jnp.array([ORDER.index(j) for j in range(4)], jnp.int32)
    return place[jnp.bitwise_xor(y, jnp.arange(4, dtype=jnp.int32))]


def on_core(kernel, at, arrays, outs):
    vmem = pl.BlockSpec(memory_space=pltpu.VMEM)
    size = sum(math.prod(a.shape) * a.dtype.itemsize for a in (*arrays, *outs))
    return pl.pallas_call(
        kernel,
        out_shape=outs,
        in_specs=[pl.BlockSpec(memory_space=pltpu.SMEM)] + [vmem] * len(arrays),
        out_specs=[vmem] * len(outs),
        compiler_params=pltpu.CompilerParams(vmem_limit_bytes=size + (8 << 20)),
        cost_estimate=pl.CostEstimate(flops=0, bytes_accessed=size, transcendentals=0),
    )(at, *arrays)


def arrange_kernel(at, here, there, tok, grad):
    m = tok.shape[0] // 8
    for d in range(4):
        for k, out in enumerate((tok, grad)):
            for i, src in enumerate((here, there)):
                to = pl.multiple_of(at[d] * 2 * m + i * m, m)
                out[pl.ds(to, m), :] = src[(2 * d + k) * m : (2 * d + k + 1) * m, :]


def pick_kernel(at, terms, own, one, two, three):
    m = own.shape[0]
    for d, out in enumerate((own, one, two, three)):
        rows = pl.ds(pl.multiple_of(at[d] * m, m), m)
        out[...] = terms[rows, :].astype(out.dtype)


def pick_sum_kernel(at, terms, other, own, one, two, three):
    m = own.shape[0]
    for d, out in enumerate((own, one, two, three)):
        rows = pl.ds(pl.multiple_of(at[d] * 2 * m, 2 * m), m)
        others = pl.ds(pl.multiple_of(at[d] * m, m), m)
        out[...] = (terms[rows, :] + other[others, :]).astype(out.dtype)


def send_core(terms, name):
    m = terms.shape[0] // 8
    return swap_core(stack([terms[(2 * i + 1) * m : (2 * i + 2) * m] for i in range(4)]), name)


def sum_x(kernel, at, arrays, m, name):
    shape = (m, arrays[0].shape[1])
    outs = [jax.ShapeDtypeStruct(shape, F32)] + [jax.ShapeDtypeStruct(shape, BF)] * 3
    own, *send = on_core(kernel, at, arrays, outs)
    return own, [shift_x(send[d - 1], d, name) for d in (2, 1, 3)]


def reduce_z(totals, name):
    n = totals[0].shape[0] // NZ
    send = lambda d: jnp.concatenate([t[d * n : (d + 1) * n] for t in totals], axis=0).astype(BF)
    got = [shift_z(send(d), d, name) for d in (1, 2, 3)]
    return [add(t[:n], *[g[i * n : (i + 1) * n] for g in got]) for i, t in enumerate(totals)]


def body(tokens, w_gate, w_up, w_down, out_grad):
    w_both = jnp.concatenate([w_gate, w_up], axis=1)
    width = w_gate.shape[1]
    half = tokens.shape[0] // 2
    at = places(lax.axis_index("row") // 2)

    near = jnp.concatenate(
        [tokens[:half], out_grad[:half], tokens[half:], out_grad[half:]], axis=0
    )
    along_z = [near] + [shift_z(near, d, "both") for d in (1, 2, 3)]

    def line(part):
        return jnp.concatenate(
            [p[i * half : (i + 1) * half] for i in (2 * part, 2 * part + 1) for p in along_z],
            axis=0,
        )

    def both_cores(own, name):
        here = stack(own)
        there = swap_core(here, name)
        out = jax.ShapeDtypeStruct((here.shape[0], here.shape[1]), BF)
        return on_core(arrange_kernel, at, [here, there], [out, out])

    def from_x(a, name):
        got = {d: shift_x(a, d, name) for d in (2, 1, 3)}
        return [a, got[1], got[2], got[3]]

    def partials(tok, grad):
        return jnp.concatenate([dot(tok, w_both, 1, 0), dot(grad, w_down, 1, 1)], axis=1)

    def send_y(part, name):
        m = part.shape[0] // 4
        return [shift_y(part[i * m : (i + 1) * m], j, name) for i, j in enumerate(ORDER[:3])]

    def own_block(tok, grad):
        m = tok.shape[0] // 4
        return partials(tok[3 * m :], grad[3 * m :])

    def middle(total):
        gate_pre, up_pre, hid_grad = (total[:, i * width : (i + 1) * width] for i in range(3))
        sigmoid_g = jax.nn.sigmoid(gate_pre)
        activated = gate_pre * sigmoid_g
        hidden = (activated * up_pre).astype(BF)
        gate_delta = hid_grad * up_pre * sigmoid_g * (1.0 + gate_pre * (1.0 - sigmoid_g))
        up_delta = hid_grad * activated
        return hidden, jnp.concatenate([gate_delta.astype(BF), up_delta.astype(BF)], axis=1)

    def spread_y(a, name):
        return [shift_y(a, j, name) for j in ORDER[:3]] + [a]

    def out_terms(hid, delta):
        return jnp.concatenate([dot(hid, w_down, 1, 0), dot(delta, w_both, 1, 1)], axis=1)

    line_a, line_b = line(0), line(1)
    tok_a, grad_a = both_cores(from_x(line_a, "a"), "a")

    a_front = dot(tok_a, w_both, 1, 0).astype(BF)
    line_b = after(line_b, a_front)
    a_got = send_y(a_front, "a_front")
    b_x = from_x(line_b, "b")

    a_back = dot(grad_a, w_down, 1, 1).astype(BF)
    a_got = after_list(a_got, *b_x, a_back)
    a_back = after(a_back, *a_got)
    a_got_h = send_y(a_back, "a_back")
    tok_b, grad_b = both_cores(after_list(b_x, a_back), "b")
    a_got = [jnp.concatenate([p, q], axis=1) for p, q in zip(a_got, a_got_h)]

    b_send = partials(tok_b, grad_b).astype(BF)
    b_send = after(b_send, *a_got)
    b_got = send_y(b_send, "b")
    a_sum = add(own_block(tok_a, after(grad_a, *a_got)), *a_got)
    a_h = swap_h(a_sum.astype(BF), "a")

    b_sum = add(own_block(tok_b, after(grad_b, *b_got)), *b_got)
    b_h = swap_h(b_sum.astype(BF), "b")
    a_h = after(a_h, b_sum)
    a_hid, a_delta = middle(a_sum + a_h.astype(F32))
    a_all = spread_y(jnp.concatenate([a_hid, a_delta], axis=1), "mid_a")
    a_hid_all = stack([a[:, :width] for a in a_all])
    a_delta_all = stack([a[:, width:] for a in a_all])

    a_terms = out_terms(a_hid_all, a_delta_all)
    b_hid, b_delta = middle(b_sum + after(b_h, a_terms).astype(F32))
    b_mid = jnp.concatenate([b_hid, b_delta], axis=1)
    b_all = spread_y(b_mid, "mid_b")
    m = a_terms.shape[0] // 4
    a_own, a_x = sum_x(pick_kernel, at, [a_terms], m, "a")
    b_all = after_list(b_all, *a_x)
    a_x = after_list(a_x, b_all[0])
    b_hid_all = stack([b[:, :width] for b in b_all])
    b_delta_all = stack([b[:, width:] for b in b_all])
    hid_all = stack([a_hid_all, b_hid_all])
    grad_all = stack([grad_a, grad_b])
    tok_all = stack([tok_a, tok_b])
    scale = 1.0 / math.sqrt(tok_all.shape[0])

    delta_all = stack([a_delta_all, b_delta_all])
    b_terms = out_terms(b_hid_all, b_delta_all)
    b_core = send_core(b_terms, "b")
    a_total = add(a_own, *a_x)
    a_core = swap_core(a_total[m // 2 :], "a")
    gate_grad = (dot(after(tok_all, b_terms), delta_all[:, :width], 0, 0) * scale).astype(BF)
    b_own, b_x = sum_x(pick_sum_kernel, at, [b_terms, after(b_core, gate_grad)], m // 2, "b")
    a_total = a_total[: m // 2] + after(a_core, b_own)
    down_grad = (dot(after(hid_all, b_own), grad_all, 0, 0) * scale).astype(BF)

    totals = [a_total, add(b_own, *after_list(b_x, down_grad))]
    out = jnp.concatenate(reduce_z(totals, "both"), axis=0)
    up_grad = (dot(after(tok_all, totals[1]), delta_all[:, width:], 0, 0) * scale).astype(BF)
    n = tokens.shape[1]
    return (
        out[:, :n].astype(BF),
        out[:, n:].astype(BF),
        gate_grad,
        up_grad,
        down_grad,
    )


def after_list(parts, *earlier):
    return list(lax.optimization_barrier((*parts, *earlier))[: len(parts)])


def solution(mesh):
    placed = (P("col", "row"), P("row", "col"), P("row", "col"), P("col", "row"), P("col", "row"))
    return jax.shard_map(
        body,
        mesh=mesh,
        in_specs=placed,
        out_specs=(
            P("col", "row"),
            P("col", "row"),
            P("row", "col"),
            P("row", "col"),
            P("col", "row"),
        ),
        check_vma=False,
    )
```

```python
import math

import jax
import jax.numpy as jnp
from jax import lax
from jax.experimental import pallas as pl
from jax.experimental.pallas import tpu as pltpu
from jax.sharding import PartitionSpec as P

BF, F32 = jnp.bfloat16, jnp.float32
NX, NZ, NY = 4, 4, 4
OTHERS = (2, 1, 3)
DEVICES = [
    (y, h, z, x, k)
    for y in range(NY)
    for h in range(2)
    for z in range(NZ)
    for x in range(NX)
    for k in range(2)
]


def flat(y, h, z, x, k):
    return ((y % NY) * 2 + h % 2) * 32 + ((z % NZ) * NX + x % NX) * 2 + k % 2


def permute(a, name, target):
    with jax.named_scope(name):
        return lax.ppermute(a, ("row", "col"), [(flat(*d), flat(*target(*d))) for d in DEVICES])


def shift_y(a, d, name):
    return permute(a, name + "_y", lambda y, h, z, x, k: (y ^ d, h, z, x, k))


def shift_z(a, d, name):
    return permute(a, name + "_z", lambda y, h, z, x, k: (y, h, z ^ d, x, k))


def swap_h(a, name):
    return permute(a, name + "_h", lambda y, h, z, x, k: (y, h + 1, z, x, k))


def swap_core(a, name):
    return permute(a, name + "_core", lambda y, h, z, x, k: (y, h, z, x, k + 1))


def shift_x(a, d, name):
    return permute(a, name + "_x", lambda y, h, z, x, k: (y, h, z, x ^ d, k))


def after(a, *earlier):
    return lax.optimization_barrier((a, *earlier))[0]


def add(*parts):
    total = parts[0].astype(F32)
    for p in parts[1:]:
        total = total + p.astype(F32)
    return total


def dot(a, b, ca, cb):
    return lax.dot_general(a, b, (((ca,), (cb,)), ((), ())), preferred_element_type=F32)


def stack(parts):
    n = parts[0].shape[0]
    out = jnp.zeros((n * len(parts), parts[0].shape[1]), parts[0].dtype)
    for i, p in enumerate(parts):
        out = lax.dynamic_update_slice(out, p, (i * n, 0))
    return out


def on_core(kernel, arrays, outs):
    vmem = pl.BlockSpec(memory_space=pltpu.VMEM)
    size = sum(math.prod(a.shape) * a.dtype.itemsize for a in (*arrays, *outs))
    return pl.pallas_call(
        kernel,
        out_shape=outs,
        in_specs=[vmem] * len(arrays),
        out_specs=[vmem] * len(outs),
        compiler_params=pltpu.CompilerParams(vmem_limit_bytes=size + (8 << 20)),
        cost_estimate=pl.CostEstimate(flops=0, bytes_accessed=size, transcendentals=0),
    )(*arrays)


def place(d):
    return (lax.axis_index("row") // 2) ^ d


def arrange_kernel(here, there, tok, grad):
    m = tok.shape[0] // 8
    for d in range(4):
        for k, out in enumerate((tok, grad)):
            for i, src in enumerate((here, there)):
                to = pl.multiple_of(place(d) * 2 * m + i * m, m)
                out[pl.ds(to, m), :] = src[(2 * d + k) * m : (2 * d + k + 1) * m, :]


def pick_kernel(terms, own, one, two, three):
    m = own.shape[0]
    for d, out in enumerate((own, one, two, three)):
        rows = pl.ds(pl.multiple_of(place(d) * m, m), m)
        out[...] = terms[rows, :].astype(out.dtype)


def pick_sum_kernel(terms, other, own, one, two, three):
    m = own.shape[0]
    for d, out in enumerate((own, one, two, three)):
        rows = pl.ds(pl.multiple_of(place(d) * 2 * m, 2 * m), m)
        others = pl.ds(pl.multiple_of(place(d) * m, m), m)
        out[...] = (terms[rows, :] + other[others, :]).astype(out.dtype)


def send_core(terms, name):
    m = terms.shape[0] // 8
    return swap_core(stack([terms[(2 * i + 1) * m : (2 * i + 2) * m] for i in range(4)]), name)


def sum_x(kernel, arrays, m, name):
    shape = (m, arrays[0].shape[1])
    outs = [jax.ShapeDtypeStruct(shape, F32)] + [jax.ShapeDtypeStruct(shape, BF)] * 3
    own, *send = on_core(kernel, arrays, outs)
    return own, [shift_x(send[d - 1], d, name) for d in OTHERS]


def send_z(total, name):
    n = total.shape[0] // 4
    low = total.astype(BF)
    return total[:n], [shift_z(low[d * n : (d + 1) * n], d, name) for d in OTHERS]


def body(tokens, w_gate, w_up, w_down, out_grad):
    w_both = jnp.concatenate([w_gate, w_up], axis=1)
    width = w_gate.shape[1]
    half = tokens.shape[0] // 2

    near = jnp.concatenate(
        [tokens[:half], out_grad[:half], tokens[half:], out_grad[half:]], axis=0
    )
    along_z = [near] + [shift_z(near, d, "both") for d in (1, 2, 3)]

    def line(part):
        return jnp.concatenate(
            [p[i * half : (i + 1) * half] for i in (2 * part, 2 * part + 1) for p in along_z],
            axis=0,
        )

    def both_cores(own, name):
        here = stack(own)
        there = swap_core(here, name)
        out = jax.ShapeDtypeStruct((here.shape[0], here.shape[1]), BF)
        return on_core(arrange_kernel, [here, there], [out, out])

    def from_x(a, name):
        got = {d: shift_x(a, d, name) for d in OTHERS}
        return [a, got[1], got[2], got[3]]

    def partials(tok, grad):
        return jnp.concatenate([dot(tok, w_both, 1, 0), dot(grad, w_down, 1, 1)], axis=1)

    def send_y(part, name):
        m = part.shape[0] // 4
        return [shift_y(part[j * m : (j + 1) * m], j, name) for j in OTHERS]

    def own_block(tok, grad):
        m = tok.shape[0] // 4
        return partials(tok[:m], grad[:m])

    def middle(total):
        gate_pre, up_pre, hid_grad = (total[:, i * width : (i + 1) * width] for i in range(3))
        sigmoid_g = jax.nn.sigmoid(gate_pre)
        activated = gate_pre * sigmoid_g
        hidden = (activated * up_pre).astype(BF)
        gate_delta = hid_grad * up_pre * sigmoid_g * (1.0 + gate_pre * (1.0 - sigmoid_g))
        up_delta = hid_grad * activated
        return hidden, jnp.concatenate([gate_delta.astype(BF), up_delta.astype(BF)], axis=1)

    def spread_y(a, name):
        got = {j: shift_y(a, j, name) for j in OTHERS}
        return [a, got[1], got[2], got[3]]

    def out_terms(hid, delta):
        return jnp.concatenate([dot(hid, w_down, 1, 0), dot(delta, w_both, 1, 1)], axis=1)

    line_a, line_b = line(0), line(1)
    tok_a, grad_a = both_cores(from_x(line_a, "a"), "a")

    a_front = dot(tok_a, w_both, 1, 0).astype(BF)
    line_b = after(line_b, a_front)
    a_got = send_y(a_front, "a_front")
    b_x = from_x(line_b, "b")

    a_back = dot(grad_a, w_down, 1, 1).astype(BF)
    a_got = after_list(a_got, *b_x, a_back)
    a_back = after(a_back, *a_got)
    a_got_h = send_y(a_back, "a_back")
    tok_b, grad_b = both_cores(after_list(b_x, a_back), "b")
    a_got = [jnp.concatenate([p, q], axis=1) for p, q in zip(a_got, a_got_h)]

    b_send = partials(tok_b, grad_b).astype(BF)
    b_send = after(b_send, *a_got)
    b_got = send_y(b_send, "b")
    a_sum = add(own_block(tok_a, after(grad_a, b_send)), *a_got)
    a_h = swap_h(a_sum.astype(BF), "a")

    b_sum = add(own_block(tok_b, after(grad_b, *b_got)), *b_got)
    b_h = swap_h(b_sum.astype(BF), "b")
    a_h = after(a_h, b_sum)
    a_hid, a_delta = middle(a_sum + a_h.astype(F32))
    a_all = spread_y(jnp.concatenate([a_hid, a_delta], axis=1), "mid_a")
    a_hid_all = stack([a[:, :width] for a in a_all])
    a_delta_all = stack([a[:, width:] for a in a_all])

    a_terms = out_terms(a_hid_all, a_delta_all)
    b_hid, b_delta = middle(b_sum + after(b_h, a_terms).astype(F32))
    b_mid = jnp.concatenate([b_hid, b_delta], axis=1)
    b_all = spread_y(b_mid, "mid_b")
    m = a_terms.shape[0] // 4
    a_own, a_x = sum_x(pick_kernel, [a_terms], m, "a")
    b_hid_all = stack([b[:, :width] for b in b_all])
    b_delta_all = stack([b[:, width:] for b in b_all])
    hid_all = stack([a_hid_all, b_hid_all])
    grad_all = stack([grad_a, grad_b])
    tok_all = stack([tok_a, tok_b])
    scale = 1.0 / math.sqrt(tok_all.shape[0])

    delta_all = stack([a_delta_all, b_delta_all])
    b_mixed = dot(b_hid_all, w_down, 1, 0)
    b_delta_all, *a_x = after_list([b_delta_all, *a_x], b_mixed)
    b_terms = jnp.concatenate([b_mixed, dot(b_delta_all, w_both, 1, 1)], axis=1)
    b_core = send_core(b_terms, "b")
    a_total = add(a_own, *a_x)
    a_core = swap_core(a_total[m // 2 :], "a")
    gate_grad = (dot(after(tok_all, b_terms), delta_all[:, :width], 0, 0) * scale).astype(BF)

    b_own, b_x = sum_x(pick_sum_kernel, [b_terms, after(b_core, gate_grad)], m // 2, "b")
    a_out, a_z = send_z(a_total[: m // 2] + after(a_core, b_own), "a")

    tok_all = after(tok_all, b_own)
    up_grad = (dot(tok_all, delta_all[:, width:], 0, 0) * scale).astype(BF)
    b_x = after_list(b_x, up_grad)
    b_total = add(b_own, *b_x)
    a_z = after_list(a_z, b_total)
    b_total = after(b_total, *a_z)
    b_out, b_z = send_z(b_total, "b")
    down_grad = (dot(after(hid_all, b_total), grad_all, 0, 0) * scale).astype(BF)
    b_z = after_list(b_z, down_grad)
    out = jnp.concatenate([add(a_out, *a_z), add(b_out, *b_z)], axis=0)
    n = tokens.shape[1]
    return (
        out[:, :n].astype(BF),
        out[:, n:].astype(BF),
        gate_grad,
        up_grad,
        down_grad,
    )


def after_list(parts, *earlier):
    return list(lax.optimization_barrier((*parts, *earlier))[: len(parts)])


def solution(mesh):
    placed = (P("col", "row"), P("row", "col"), P("row", "col"), P("col", "row"), P("col", "row"))
    return jax.shard_map(
        body,
        mesh=mesh,
        in_specs=placed,
        out_specs=(
            P("col", "row"),
            P("col", "row"),
            P("row", "col"),
            P("row", "col"),
            P("col", "row"),
        ),
        check_vma=False,
    )
```

```python
import math

import jax
import jax.numpy as jnp
from jax import lax
from jax.experimental import pallas as pl
from jax.experimental.pallas import tpu as pltpu
from jax.sharding import PartitionSpec as P

BF, F32 = jnp.bfloat16, jnp.float32
NX, NZ, NY = 4, 4, 4
OTHERS = (2, 1, 3)
DEVICES = [
    (y, h, z, x, k)
    for y in range(NY)
    for h in range(2)
    for z in range(NZ)
    for x in range(NX)
    for k in range(2)
]


def flat(y, h, z, x, k):
    return ((y % NY) * 2 + h % 2) * 32 + ((z % NZ) * NX + x % NX) * 2 + k % 2


def permute(a, name, target):
    with jax.named_scope(name):
        return lax.ppermute(a, ("row", "col"), [(flat(*d), flat(*target(*d))) for d in DEVICES])


def shift_y(a, d, name):
    return permute(a, name + "_y", lambda y, h, z, x, k: (y ^ d, h, z, x, k))


def shift_z(a, d, name):
    return permute(a, name + "_z", lambda y, h, z, x, k: (y, h, z ^ d, x, k))


def swap_h(a, name):
    return permute(a, name + "_h", lambda y, h, z, x, k: (y, h + 1, z, x, k))


def swap_core(a, name):
    return permute(a, name + "_core", lambda y, h, z, x, k: (y, h, z, x, k + 1))


def shift_x(a, d, name):
    return permute(a, name + "_x", lambda y, h, z, x, k: (y, h, z, x ^ d, k))


def after(a, *earlier):
    return lax.optimization_barrier((a, *earlier))[0]


def add(*parts):
    total = parts[0].astype(F32)
    for p in parts[1:]:
        total = total + p.astype(F32)
    return total


def dot(a, b, ca, cb):
    return lax.dot_general(a, b, (((ca,), (cb,)), ((), ())), preferred_element_type=F32)


def stack(parts):
    n = parts[0].shape[0]
    out = jnp.zeros((n * len(parts), parts[0].shape[1]), parts[0].dtype)
    for i, p in enumerate(parts):
        out = lax.dynamic_update_slice(out, p, (i * n, 0))
    return out


def on_core(kernel, arrays, outs):
    vmem = pl.BlockSpec(memory_space=pltpu.VMEM)
    size = sum(math.prod(a.shape) * a.dtype.itemsize for a in (*arrays, *outs))
    return pl.pallas_call(
        kernel,
        out_shape=outs,
        in_specs=[vmem] * len(arrays),
        out_specs=[vmem] * len(outs),
        compiler_params=pltpu.CompilerParams(vmem_limit_bytes=size + (8 << 20)),
        cost_estimate=pl.CostEstimate(flops=0, bytes_accessed=size, transcendentals=0),
    )(*arrays)


def place(d):
    return (lax.axis_index("row") // 2) ^ d


def arrange_kernel(here, there, tok, grad):
    m = tok.shape[0] // 8
    for d in range(4):
        for k, out in enumerate((tok, grad)):
            for i, src in enumerate((here, there)):
                to = pl.multiple_of(place(d) * 2 * m + i * m, m)
                out[pl.ds(to, m), :] = src[(2 * d + k) * m : (2 * d + k + 1) * m, :]


def pick_kernel(terms, own, one, two, three):
    m = own.shape[0]
    for d, out in enumerate((own, one, two, three)):
        rows = pl.ds(pl.multiple_of(place(d) * m, m), m)
        out[...] = terms[rows, :].astype(out.dtype)


def pick_sum_kernel(terms, other, own, one, two, three):
    m = own.shape[0]
    for d, out in enumerate((own, one, two, three)):
        rows = pl.ds(pl.multiple_of(place(d) * 2 * m, 2 * m), m)
        others = pl.ds(pl.multiple_of(place(d) * m, m), m)
        out[...] = (terms[rows, :] + other[others, :]).astype(out.dtype)


def send_core(terms, name):
    m = terms.shape[0] // 8
    return swap_core(stack([terms[(2 * i + 1) * m : (2 * i + 2) * m] for i in range(4)]), name)


def sum_x(kernel, arrays, m, name):
    shape = (m, arrays[0].shape[1])
    outs = [jax.ShapeDtypeStruct(shape, F32)] + [jax.ShapeDtypeStruct(shape, BF)] * 3
    own, *send = on_core(kernel, arrays, outs)
    return own, [shift_x(send[d - 1], d, name) for d in OTHERS]


def send_z(total, name):
    n = total.shape[0] // 4
    low = total.astype(BF)
    return total[:n], [shift_z(low[d * n : (d + 1) * n], d, name) for d in OTHERS]


def body(tokens, w_gate, w_up, w_down, out_grad):
    w_both = jnp.concatenate([w_gate, w_up], axis=1)
    width = w_gate.shape[1]
    half = tokens.shape[0] // 2

    near = jnp.concatenate(
        [tokens[:half], out_grad[:half], tokens[half:], out_grad[half:]], axis=0
    )
    along_z = [near] + [shift_z(near, d, "both") for d in (1, 2, 3)]

    def line(part):
        return jnp.concatenate(
            [p[i * half : (i + 1) * half] for i in (2 * part, 2 * part + 1) for p in along_z],
            axis=0,
        )

    def both_cores(own, name):
        here = stack(own)
        there = swap_core(here, name)
        out = jax.ShapeDtypeStruct((here.shape[0], here.shape[1]), BF)
        return on_core(arrange_kernel, [here, there], [out, out])

    def from_x(a, name):
        got = {d: shift_x(a, d, name) for d in OTHERS}
        return [a, got[1], got[2], got[3]]

    def partials(tok, grad):
        return jnp.concatenate([dot(tok, w_both, 1, 0), dot(grad, w_down, 1, 1)], axis=1)

    def send_y(part, name):
        m = part.shape[0] // 4
        return [shift_y(part[j * m : (j + 1) * m], j, name) for j in OTHERS]

    def own_block(tok, grad):
        m = tok.shape[0] // 4
        return partials(tok[:m], grad[:m])

    def middle(total):
        gate_pre, up_pre, hid_grad = (total[:, i * width : (i + 1) * width] for i in range(3))
        sigmoid_g = jax.nn.sigmoid(gate_pre)
        activated = gate_pre * sigmoid_g
        hidden = (activated * up_pre).astype(BF)
        gate_delta = hid_grad * up_pre * sigmoid_g * (1.0 + gate_pre * (1.0 - sigmoid_g))
        up_delta = hid_grad * activated
        return hidden, jnp.concatenate([gate_delta.astype(BF), up_delta.astype(BF)], axis=1)

    def spread_y(a, name):
        one, three = shift_y(a, 1, name), shift_y(a, 3, name)
        n = a.shape[0] // 2
        far = [shift_y(three[:n], 1, name + "_far"), shift_y(one[n:], 3, name + "_far")]
        return [a, one, stack(far), three]

    def out_terms(hid, delta):
        return jnp.concatenate([dot(hid, w_down, 1, 0), dot(delta, w_both, 1, 1)], axis=1)

    line_a, line_b = line(0), line(1)
    tok_a, grad_a = both_cores(from_x(line_a, "a"), "a")

    a_front = dot(tok_a, w_both, 1, 0).astype(BF)
    line_b = after(line_b, a_front)
    a_got = send_y(a_front, "a_front")
    b_x = from_x(line_b, "b")

    a_back = dot(grad_a, w_down, 1, 1).astype(BF)
    a_got = after_list(a_got, *b_x, a_back)
    a_back = after(a_back, *a_got)
    a_got_h = send_y(a_back, "a_back")
    tok_b, grad_b = both_cores(after_list(b_x, a_back), "b")
    a_got = [jnp.concatenate([p, q], axis=1) for p, q in zip(a_got, a_got_h)]

    b_send = partials(tok_b, grad_b).astype(BF)
    b_got = send_y(b_send, "b")
    a_sum = add(own_block(tok_a, after(grad_a, b_send)), *a_got)
    a_h = swap_h(a_sum.astype(BF), "a")

    b_sum = add(own_block(tok_b, after(grad_b, *b_got)), *b_got)
    b_h = swap_h(b_sum.astype(BF), "b")
    a_h = after(a_h, b_sum)
    a_hid, a_delta = middle(a_sum + a_h.astype(F32))
    a_all = spread_y(jnp.concatenate([a_hid, a_delta], axis=1), "mid_a")
    a_hid_all = stack([a[:, :width] for a in a_all])
    a_delta_all = stack([a[:, width:] for a in a_all])

    a_terms = out_terms(a_hid_all, a_delta_all)
    b_hid, b_delta = middle(b_sum + after(b_h, a_terms).astype(F32))
    b_mid = jnp.concatenate([b_hid, b_delta], axis=1)
    b_all = spread_y(b_mid, "mid_b")
    m = a_terms.shape[0] // 4
    a_own, a_x = sum_x(pick_kernel, [a_terms], m, "a")
    b_hid_all = stack([b[:, :width] for b in b_all])
    b_delta_all = stack([b[:, width:] for b in b_all])
    hid_all = stack([a_hid_all, b_hid_all])
    grad_all = stack([grad_a, grad_b])
    tok_all = stack([tok_a, tok_b])
    scale = 1.0 / math.sqrt(tok_all.shape[0])

    delta_all = stack([a_delta_all, b_delta_all])
    b_mixed = dot(b_hid_all, w_down, 1, 0)
    b_delta_all, *a_x = after_list([b_delta_all, *a_x], b_mixed)
    b_terms = jnp.concatenate([b_mixed, dot(b_delta_all, w_both, 1, 1)], axis=1)
    b_core = send_core(b_terms, "b")
    a_total = add(a_own, *a_x)
    a_core = swap_core(a_total[m // 2 :], "a")
    gate_grad = (dot(after(tok_all, b_terms), delta_all[:, :width], 0, 0) * scale).astype(BF)

    b_own, b_x = sum_x(pick_sum_kernel, [b_terms, after(b_core, gate_grad)], m // 2, "b")
    a_out, a_z = send_z(a_total[: m // 2] + after(a_core, b_own), "a")

    tok_all = after(tok_all, b_own)
    up_grad = (dot(tok_all, delta_all[:, width:], 0, 0) * scale).astype(BF)
    b_x = after_list(b_x, up_grad)
    b_total = add(b_own, *b_x)
    down_grad = (dot(after(hid_all, b_total), grad_all, 0, 0) * scale).astype(BF)
    a_total = after(add(a_out, *after_list(a_z, b_total)), b_total)
    b_total = after(b_total, a_total)
    b_out, b_z = send_z(b_total, "b")
    b_z = after_list(b_z, down_grad)
    out = jnp.concatenate([a_total, add(b_out, *b_z)], axis=0)
    n = tokens.shape[1]
    return (
        out[:, :n].astype(BF),
        out[:, n:].astype(BF),
        gate_grad,
        up_grad,
        down_grad,
    )


def after_list(parts, *earlier):
    return list(lax.optimization_barrier((*parts, *earlier))[: len(parts)])


def solution(mesh):
    placed = (P("col", "row"), P("row", "col"), P("row", "col"), P("col", "row"), P("col", "row"))
    return jax.shard_map(
        body,
        mesh=mesh,
        in_specs=placed,
        out_specs=(
            P("col", "row"),
            P("col", "row"),
            P("row", "col"),
            P("row", "col"),
            P("col", "row"),
        ),
        check_vma=False,
    )
```

```python
import math

import jax
import jax.numpy as jnp
from jax import lax
from jax.experimental import pallas as pl
from jax.experimental.pallas import tpu as pltpu
from jax.sharding import PartitionSpec as P

BF, F32 = jnp.bfloat16, jnp.float32
NX, NZ, NY = 4, 4, 4
OTHERS = (2, 1, 3)
DEVICES = [
    (y, h, z, x, k)
    for y in range(NY)
    for h in range(2)
    for z in range(NZ)
    for x in range(NX)
    for k in range(2)
]


def flat(y, h, z, x, k):
    return ((y % NY) * 2 + h % 2) * 32 + ((z % NZ) * NX + x % NX) * 2 + k % 2


def permute(a, name, target):
    with jax.named_scope(name):
        return lax.ppermute(a, ("row", "col"), [(flat(*d), flat(*target(*d))) for d in DEVICES])


def shift_y(a, d, name):
    return permute(a, name + "_y", lambda y, h, z, x, k: (y ^ d, h, z, x, k))


def shift_z(a, d, name):
    return permute(a, name + "_z", lambda y, h, z, x, k: (y, h, z ^ d, x, k))


def swap_h(a, name):
    return permute(a, name + "_h", lambda y, h, z, x, k: (y, h + 1, z, x, k))


def swap_core(a, name):
    return permute(a, name + "_core", lambda y, h, z, x, k: (y, h, z, x, k + 1))


def shift_x(a, d, name):
    return permute(a, name + "_x", lambda y, h, z, x, k: (y, h, z, x ^ d, k))


def after(a, *earlier):
    return lax.optimization_barrier((a, *earlier))[0]


def add(*parts):
    total = parts[0].astype(F32)
    for p in parts[1:]:
        total = total + p.astype(F32)
    return total


def dot(a, b, ca, cb):
    return lax.dot_general(a, b, (((ca,), (cb,)), ((), ())), preferred_element_type=F32)


def stack(parts):
    n = parts[0].shape[0]
    out = jnp.zeros((n * len(parts), parts[0].shape[1]), parts[0].dtype)
    for i, p in enumerate(parts):
        out = lax.dynamic_update_slice(out, p, (i * n, 0))
    return out


def on_core(kernel, arrays, outs):
    vmem = pl.BlockSpec(memory_space=pltpu.VMEM)
    size = sum(math.prod(a.shape) * a.dtype.itemsize for a in (*arrays, *outs))
    return pl.pallas_call(
        kernel,
        out_shape=outs,
        in_specs=[vmem] * len(arrays),
        out_specs=[vmem] * len(outs),
        compiler_params=pltpu.CompilerParams(vmem_limit_bytes=size + (8 << 20)),
        cost_estimate=pl.CostEstimate(flops=0, bytes_accessed=size, transcendentals=0),
    )(*arrays)


def place(d):
    return (lax.axis_index("row") // 2) ^ d


def arrange_kernel(here, there, tok, grad):
    m = tok.shape[0] // 8
    for d in range(4):
        for k, out in enumerate((tok, grad)):
            for i, src in enumerate((here, there)):
                to = pl.multiple_of(place(d) * 2 * m + i * m, m)
                out[pl.ds(to, m), :] = src[(2 * d + k) * m : (2 * d + k + 1) * m, :]


def pick_kernel(terms, own, one, two, three):
    m = own.shape[0]
    for d, out in enumerate((own, one, two, three)):
        rows = pl.ds(pl.multiple_of(place(d) * m, m), m)
        out[...] = terms[rows, :].astype(out.dtype)


def pick_sum_kernel(terms, other, own, one, two, three):
    m = own.shape[0]
    for d, out in enumerate((own, one, two, three)):
        rows = pl.ds(pl.multiple_of(place(d) * 2 * m, 2 * m), m)
        others = pl.ds(pl.multiple_of(place(d) * m, m), m)
        out[...] = (terms[rows, :] + other[others, :]).astype(out.dtype)


def send_core(terms, name):
    m = terms.shape[0] // 8
    return swap_core(stack([terms[(2 * i + 1) * m : (2 * i + 2) * m] for i in range(4)]), name)


def sum_x(kernel, arrays, m, name):
    shape = (m, arrays[0].shape[1])
    outs = [jax.ShapeDtypeStruct(shape, F32)] + [jax.ShapeDtypeStruct(shape, BF)] * 3
    own, *send = on_core(kernel, arrays, outs)
    return own, [shift_x(send[d - 1], d, name) for d in OTHERS]


def send_z(total, name):
    n = total.shape[0] // 4
    low = total.astype(BF)
    return total[:n], [shift_z(low[d * n : (d + 1) * n], d, name) for d in OTHERS]


def body(tokens, w_gate, w_up, w_down, out_grad):
    w_both = jnp.concatenate([w_gate, w_up], axis=1)
    width = w_gate.shape[1]
    half = tokens.shape[0] // 2

    near = jnp.concatenate(
        [tokens[:half], out_grad[:half], tokens[half:], out_grad[half:]], axis=0
    )
    along_z = [near] + [shift_z(near, d, "both") for d in (1, 2, 3)]

    def line(part):
        return jnp.concatenate(
            [p[i * half : (i + 1) * half] for i in (2 * part, 2 * part + 1) for p in along_z],
            axis=0,
        )

    def both_cores(own, name):
        here = stack(own)
        there = swap_core(here, name)
        out = jax.ShapeDtypeStruct((here.shape[0], here.shape[1]), BF)
        return on_core(arrange_kernel, [here, there], [out, out])

    def from_x(a, name):
        got = {d: shift_x(a, d, name) for d in OTHERS}
        return [a, got[1], got[2], got[3]]

    def partials(tok, grad):
        return jnp.concatenate([dot(tok, w_both, 1, 0), dot(grad, w_down, 1, 1)], axis=1)

    def send_y(part, name):
        m = part.shape[0] // 4
        return [shift_y(part[j * m : (j + 1) * m], j, name) for j in OTHERS]

    def own_block(tok, grad):
        m = tok.shape[0] // 4
        return partials(tok[:m], grad[:m])

    def middle(total):
        gate_pre, up_pre, hid_grad = (total[:, i * width : (i + 1) * width] for i in range(3))
        sigmoid_g = jax.nn.sigmoid(gate_pre)
        activated = gate_pre * sigmoid_g
        hidden = (activated * up_pre).astype(BF)
        gate_delta = hid_grad * up_pre * sigmoid_g * (1.0 + gate_pre * (1.0 - sigmoid_g))
        up_delta = hid_grad * activated
        return hidden, jnp.concatenate([gate_delta.astype(BF), up_delta.astype(BF)], axis=1)

    def spread_y(a, name):
        one, three = shift_y(a, 1, name), shift_y(a, 3, name)
        n = a.shape[0] // 2
        far = [shift_y(three[:n], 1, name + "_far"), shift_y(one[n:], 3, name + "_far")]
        return [a, one, stack(far), three]

    def out_terms(hid, delta):
        return jnp.concatenate([dot(hid, w_down, 1, 0), dot(delta, w_both, 1, 1)], axis=1)

    line_a, line_b = line(0), line(1)
    tok_a, grad_a = both_cores(from_x(line_a, "a"), "a")

    a_front = dot(tok_a, w_both, 1, 0).astype(BF)
    line_b = after(line_b, a_front)
    a_got = send_y(a_front, "a_front")
    b_x = from_x(line_b, "b")

    a_back = dot(grad_a, w_down, 1, 1).astype(BF)
    a_got = after_list(a_got, *b_x, a_back)
    a_back = after(a_back, *a_got)
    a_got_h = send_y(a_back, "a_back")
    tok_b, grad_b = both_cores(after_list(b_x, a_back), "b")

    b_send = partials(tok_b, grad_b).astype(BF)
    b_got = send_y(b_send, "b")
    n = tok_a.shape[0] // 4
    a_front = add(dot(after(tok_a, b_send)[:n], w_both, 1, 0), *a_got)
    a_front_h = swap_h(a_front.astype(BF), "a_front")
    a_back = add(dot(after(grad_a, b_send)[:n], w_down, 1, 1), *a_got_h)
    a_back_h = swap_h(after(a_back.astype(BF), a_front_h), "a_back")
    a_sum = jnp.concatenate([a_front, a_back], axis=1)

    b_sum = add(own_block(tok_b, after(grad_b, *b_got)), *b_got)
    b_h = swap_h(b_sum.astype(BF), "b")
    a_h = jnp.concatenate(after_list([a_front_h, a_back_h], b_sum), axis=1)
    a_hid, a_delta = middle(a_sum + a_h.astype(F32))
    a_all = spread_y(jnp.concatenate([a_hid, a_delta], axis=1), "mid_a")
    a_hid_all = stack([a[:, :width] for a in a_all])
    a_delta_all = stack([a[:, width:] for a in a_all])

    a_terms = out_terms(a_hid_all, a_delta_all)
    b_hid, b_delta = middle(b_sum + after(b_h, a_terms).astype(F32))
    b_mid = jnp.concatenate([b_hid, b_delta], axis=1)
    b_all = spread_y(b_mid, "mid_b")
    m = a_terms.shape[0] // 4
    a_own, a_x = sum_x(pick_kernel, [a_terms], m, "a")
    b_hid_all = stack([b[:, :width] for b in b_all])
    b_delta_all = stack([b[:, width:] for b in b_all])
    hid_all = stack([a_hid_all, b_hid_all])
    grad_all = stack([grad_a, grad_b])
    tok_all = stack([tok_a, tok_b])
    scale = 1.0 / math.sqrt(tok_all.shape[0])

    delta_all = stack([a_delta_all, b_delta_all])
    b_mixed = dot(b_hid_all, w_down, 1, 0)
    b_delta_all, *a_x = after_list([b_delta_all, *a_x], b_mixed)
    b_terms = jnp.concatenate([b_mixed, dot(b_delta_all, w_both, 1, 1)], axis=1)
    b_core = send_core(b_terms, "b")
    a_total = add(a_own, *a_x)
    a_core = swap_core(a_total[m // 2 :], "a")
    gate_grad = (dot(after(tok_all, b_terms), delta_all[:, :width], 0, 0) * scale).astype(BF)

    b_own, b_x = sum_x(pick_sum_kernel, [b_terms, after(b_core, gate_grad)], m // 2, "b")
    a_out, a_z = send_z(a_total[: m // 2] + after(a_core, b_own), "a")

    tok_all = after(tok_all, b_own)
    up_grad = (dot(tok_all, delta_all[:, width:], 0, 0) * scale).astype(BF)
    b_x = after_list(b_x, up_grad)
    b_total = add(b_own, *b_x)
    down_grad = (dot(after(hid_all, b_total), grad_all, 0, 0) * scale).astype(BF)
    a_total = after(add(a_out, *after_list(a_z, b_total)), b_total)
    b_total = after(b_total, a_total)
    b_out, b_z = send_z(b_total, "b")
    b_z = after_list(b_z, down_grad)
    out = jnp.concatenate([a_total, add(b_out, *b_z)], axis=0)
    n = tokens.shape[1]
    return (
        out[:, :n].astype(BF),
        out[:, n:].astype(BF),
        gate_grad,
        up_grad,
        down_grad,
    )


def after_list(parts, *earlier):
    return list(lax.optimization_barrier((*parts, *earlier))[: len(parts)])


def solution(mesh):
    placed = (P("col", "row"), P("row", "col"), P("row", "col"), P("col", "row"), P("col", "row"))
    return jax.shard_map(
        body,
        mesh=mesh,
        in_specs=placed,
        out_specs=(
            P("col", "row"),
            P("col", "row"),
            P("row", "col"),
            P("row", "col"),
            P("col", "row"),
        ),
        check_vma=False,
    )
```
